512 devices in a mesh: band: 32 (over x, z_lo, core), plane: 16 (over y, z_hi).
Axes of the slice: x: 4, y: 8, z: 8 (z_hi: 2, z_lo: 4; z = z_hi * 4 + z_lo), core: 2. Of those that a mesh axis runs over, the one named last changes fastest.
Arguments:
- orbitals: float32 [64, 128, 128, 128], P('band', 'plane'), may hold values from -6 to 6
- plan: int32 [2], replicated, may hold values from 0 to 63
- cutoff_mask: int32 [128, 128, 128], P(None, 'plane'), may hold values 0 or 1
Outputs:
- exchange_action: float32 [64, 128, 128, 128], P('band', 'plane')
The draws below stay inside these ranges and needn't reach their ends.
All inputs are finite; a program needn't handle non-finite values. No bound on the sum of `cutoff_mask` on one device may be relied on, other than what follows from the above.
Results may differ from the reference program's by a relative error of at most 0.00027.
Values sent between devices are 32-bit elements; how exact they have to be, the bound alone decides.
A program may use at most 64 MiB of HBM per device.

```python
import math
import jax
import jax.numpy as jnp
from jax import lax

N = 128
STEPS = 2
NB = 64


def touch_ends(entries, rng, low, largest):
    longest = entries.shape.index(max(entries.shape))
    spots = []
    for shift in (0, 1):
        where = [jax.random.randint(jax.random.fold_in(rng, axis), (), 0, length) for axis, length in enumerate(entries.shape)]
        where[longest] = (where[longest] + shift) % entries.shape[longest]
        spots.append(tuple(where))
    return entries.at[spots[0]].set(low).at[spots[1]].set(largest)


def levels(key, shape, split, least, largest):
    level = 1.0
    for axis_at, parts in split:
        draws = jax.random.uniform(jax.random.fold_in(jax.random.fold_in(key, 6), axis_at), (parts,), jnp.float32, least / len(split), largest / len(split))
        level = level * jnp.repeat(jnp.exp(draws), shape[axis_at] // parts).reshape((-1,) + (1,) * (len(shape) - 1 - axis_at))
    return level


def gaussian(own_key, shape, width, reach, shards=(), held_as=jnp.bfloat16):
    gain = levels(own_key, shape, shards, -0.22, 0.18) if shards else 1.0
    array = jax.random.normal(own_key, shape, jnp.float32) * width * gain
    return jnp.minimum(jnp.maximum(array, -reach), reach).astype(held_as)


def setup_inputs(seed: int = 0) -> dict:
    key_of = jax.random.split(jax.random.key(seed), 4)
    orbitals = gaussian(key_of[0], (NB, N, N, N), 1.0, 6.0, ((0, 32), (1, 16)), jnp.float32)
    plan = jax.random.randint(key_of[1], (STEPS,), 0, NB).astype(jnp.int32)
    cutoff_mask = touch_ends((jax.random.randint(key_of[2], (N, N, N), 0, 4) < 3).astype(jnp.int32), jax.random.fold_in(key_of[2], 1), 0, 1)
    return dict(orbitals=orbitals, plan=plan, cutoff_mask=cutoff_mask)


def cas_table(size):
    index = jnp.arange(size, dtype=jnp.int32)
    product = (index[:, None] * index[None, :]) % size
    angle = product.astype(jnp.float32) * (2.0 * math.pi / size)
    return jnp.cos(angle) + jnp.sin(angle)


def screened_kernel(size, offset, count):
    first = jnp.arange(size, dtype=jnp.int32)
    second = offset + jnp.arange(count, dtype=jnp.int32)
    signed_a = jnp.where(first < size // 2, first, first - size).astype(jnp.float32)
    signed_b = jnp.where(second < size // 2, second, second - size).astype(jnp.float32)
    wave_a = signed_a * (2.0 * math.pi / 41.04)
    wave_b = signed_b * (2.0 * math.pi / 41.04)
    wave_c = signed_a * (2.0 * math.pi / 20.52)
    squared = wave_a[:, None, None] ** 2 + wave_b[None, :, None] ** 2 + wave_c[None, None, :] ** 2
    omega = 0.106
    safe = jnp.where(squared > 0, squared, 1.0)
    screened = -4.0 * math.pi * (1.0 - jnp.exp(-safe / (4.0 * omega * omega))) / safe
    return jnp.where(squared > 0, screened, -math.pi / (omega * omega))


def along_last(field, table):
    return jnp.einsum('bxyz,kz->bxyk', field, table, precision=lax.Precision.HIGHEST)


def along_second(field, table):
    return jnp.einsum('bxyz,ky->bxkz', field, table, precision=lax.Precision.HIGHEST)


def along_first(field, table):
    return jnp.einsum('bxyz,kx->bkyz', field, table, precision=lax.Precision.HIGHEST)


def reference(orbitals, plan, cutoff_mask):
    size = orbitals.shape[1]
    table = cas_table(size)
    kernel = screened_kernel(size, 0, size) * cutoff_mask.astype(jnp.float32)
    scale = 1.0 / (size * size * size)
    total = jnp.zeros(orbitals.shape, jnp.float32)
    for step in range(STEPS):
        phi = lax.dynamic_index_in_dim(orbitals, plan[step].astype(jnp.int32), 0, keepdims=False)

        def one_band(band):
            pair = (band * phi)[None]
            spectrum = along_first(along_second(along_last(pair, table), table), table)
            filtered = kernel[None] * spectrum
            back = along_last(along_second(along_first(filtered, table), table), table) * scale
            return phi * back[0]

        total = total + lax.map(one_band, orbitals)
    return total
```

```python
import functools
import math

import jax
import jax.numpy as jnp
import numpy as np
from jax import lax
from jax.experimental import pallas as pl
from jax.experimental.pallas import tpu as pltpu
from jax.sharding import PartitionSpec as P

MESH = pl.DeviceIdType.MESH
F32 = jnp.float32
BF16 = jnp.bfloat16
OMEGA = 0.106


def cas_table(size):
    index = np.arange(size, dtype=np.int64)
    angle = (index[:, None] * index[None, :] % size) * (2.0 * math.pi / size)
    return (np.cos(angle) + np.sin(angle)).astype(np.float32)


def split(value):
    high = value.astype(BF16)
    low = (value - high.astype(F32)).astype(BF16)
    return high, low


def product(left, right):
    a = jnp.concatenate([left[0], left[1], left[0]], axis=1)
    b = jnp.concatenate([right[0], right[0], right[1]], axis=0)
    return jnp.dot(a, b, preferred_element_type=F32)


def kernel(
    bands, planes, steps, size, slab,
    plan_ref, orb_ref, mask_ref, table_ref, out_ref,
    filt, cand, mixed, crossed, scattered, phi, sent, landed, filtered, returned,
    core_send, core_recv, scat_send, scat_recv, gath_send, gath_recv, half_send, half_recv,
    fwd_send, fwd_recv, back_send, back_recv,
):
    band = lax.axis_index("band")
    plane = lax.axis_index("plane")
    core = lax.rem(band, 2)
    chip = band // 2
    chips = bands // 2
    rings = planes // 2
    y = plane // 2
    zh = lax.rem(plane, 2)
    half = slab // 2 * size
    piece = half // chips

    order = []
    for far in sorted(range(1, rings), key=lambda d: -min(d, rings - d)):
        order += [(far, 1), (far, 0)]
    order.append((0, 1))

    def partner(far, other):
        return lax.rem(y + far, rings) * 2 + lax.rem(zh + other, 2)

    others = [(lax.rem(chip + k, chips) * 2 + core, plane) for k in range(1, chips)]
    twin = (chip * 2 + 1 - core, plane)

    barrier = pltpu.get_barrier_semaphore()
    greeted = [twin] + others + [(band, partner(*o)) for o in order]
    for device in greeted:
        pl.semaphore_signal(barrier, inc=1, device_id=device, device_id_type=MESH)

    row = lax.broadcasted_iota(jnp.int32, (size, size), 0)
    col = lax.broadcasted_iota(jnp.int32, (size, size), 1)

    def wave(index, cell):
        return jnp.where(index < size // 2, index, index - size).astype(F32) * (2.0 * math.pi / cell)

    wave_ac = wave(row, 41.04) ** 2 + wave(col, 20.52) ** 2

    def screen(k, _):
        second = plane * slab + k
        wave_b = wave(jnp.full((size, size), second, jnp.int32), 41.04)
        squared = wave_ac + wave_b * wave_b
        safe = jnp.where(squared > 0, squared, 1.0)
        screened = -4.0 * math.pi * (1.0 - jnp.exp(-safe / (4.0 * OMEGA * OMEGA))) / safe
        screened = jnp.where(squared > 0, screened, -math.pi / (OMEGA * OMEGA))
        keep = mask_ref[pl.ds(k, size, stride=slab), :].astype(F32)
        filt[k] = screened * keep * (1.0 / (size * size * size))
        return _

    lax.fori_loop(0, slab, screen, 0)
    for s in range(steps):
        first = (plan_ref[s] == 2 * band).astype(F32)
        second = (plan_ref[s] == 2 * band + 1).astype(F32)
        cand[s] = orb_ref[0] * first + orb_ref[1] * second

    pl.semaphore_wait(barrier, len(greeted))

    def copy(src, dst, send, recv, device):
        return pltpu.make_async_remote_copy(
            src_ref=src, dst_ref=dst, send_sem=send, recv_sem=recv, device_id=device, device_id_type=MESH
        )

    mine = pl.ds(pl.multiple_of(core * half, half), half)
    theirs = pl.ds(pl.multiple_of((1 - core) * half, half), half)

    def core_copy(s):
        return copy(cand.at[s, theirs], crossed.at[s], core_send.at[s], core_recv.at[s], twin)

    def chunk(k):
        return pl.ds(pl.multiple_of(k * piece, piece), piece)

    def scatter_copy(s, k):
        target = lax.rem(chip + k, chips)
        return copy(
            mixed.at[s, chunk(target)], scattered.at[s, chip], scat_send.at[s, k], scat_recv.at[s, k], others[k - 1]
        )

    def gather_copy(s, k):
        where = pl.ds(pl.multiple_of(core * half + chip * piece, piece), piece)
        return copy(phi.at[s, where], phi.at[s, where], gath_send.at[s, k], gath_recv.at[s, k], others[k - 1])

    def half_copy(s):
        return copy(phi.at[s, mine], phi.at[s, mine], half_send.at[s], half_recv.at[s], twin)

    def scatter(s):
        core_copy(s).wait_recv()
        mixed[s] = cand[s, mine] + crossed[s]
        for k in range(1, chips):
            scatter_copy(s, k).start()
        scattered[s, chip] = mixed[s, chunk(chip)]

    def gather(s):
        for k in range(1, chips):
            scatter_copy(s, k).wait_recv()
        total = scattered[s, 0]
        for k in range(1, chips):
            total = total + scattered[s, k]
        phi[s, pl.ds(pl.multiple_of(core * half + chip * piece, piece), piece)] = total
        for k in range(1, chips):
            gather_copy(s, k).start()

    def exchange(s):
        for k in range(1, chips):
            gather_copy(s, k).wait_recv()
        half_copy(s).start()

    table = split(table_ref[...])

    def forward_copy(s, b, k):
        q = partner(*order[k])
        return copy(
            sent.at[s, b, :, pl.ds(pl.multiple_of(q * slab, slab), slab)],
            landed.at[s, b, pl.ds(pl.multiple_of(plane * slab, slab), slab)],
            fwd_send.at[s, b, k], fwd_recv.at[s, b, k], (band, q),
        )

    def backward_copy(s, b, k):
        q = partner(*order[k])
        return copy(
            filtered.at[s, b, pl.ds(pl.multiple_of(q * slab, slab), slab)],
            returned.at[s, b, :, pl.ds(pl.multiple_of(plane * slab, slab), slab)],
            back_send.at[s, b, k], back_recv.at[s, b, k], (band, q),
        )

    own = pl.ds(pl.multiple_of(plane * slab, slab), slab)

    def pair(s, b):
        def one(x, _):
            rows = pl.ds(pl.multiple_of(x * size, size), size)
            field = orb_ref[b, rows] * phi[s, rows]
            field = product(split(field), table)
            sent[s, b, x] = product(table, split(field))
            return _

        lax.fori_loop(0, slab, one, 0)
        for k in range(len(order)):
            forward_copy(s, b, k).start()
        landed[s, b, own] = sent[s, b, :, own]

    def middle(s, b):
        for k in range(len(order)):
            forward_copy(s, b, k).wait_recv()
        source = landed.at[s, b].reshape(size * slab, size)
        target = filtered.at[s, b].reshape(size * slab, size)

        def one(k, _):
            field = source[pl.ds(k, size, stride=slab), :]
            field = product(table, split(field)) * filt[k]
            target[pl.ds(k, size, stride=slab), :] = product(table, split(field))
            return _

        lax.fori_loop(0, slab, one, 0)
        for k in range(len(order)):
            backward_copy(s, b, k).start()
        returned[s, b, :, own] = filtered[s, b, own]

    def last(s, b):
        for k in range(len(order)):
            backward_copy(s, b, k).wait_recv()

        def one(x, _):
            rows = pl.ds(pl.multiple_of(x * size, size), size)
            field = product(table, split(returned[s, b, x]))
            field = product(split(field), table) * phi[s, rows]
            if s == 0:
                out_ref[b, rows] = field
            else:
                out_ref[b, rows] += field
            return _

        lax.fori_loop(0, slab, one, 0)

    units = [(s, b) for s in range(steps) for b in range(2)]
    for s in range(steps):
        core_copy(s).start()
    for s in range(steps):
        scatter(s)
    for s in range(steps):
        gather(s)
    exchange(0)
    for s in range(steps):
        half_copy(s).wait_recv()
        pair(s, 0)
        if s + 1 < steps:
            exchange(s + 1)
        pair(s, 1)
    for unit in units:
        middle(*unit)
    for unit in units:
        last(*unit)

    for s in range(steps):
        core_copy(s).wait_send()
        half_copy(s).wait_send()
        for k in range(1, chips):
            scatter_copy(s, k).wait_send()
            gather_copy(s, k).wait_send()
    for s, b in units:
        for k in range(len(order)):
            forward_copy(s, b, k).wait_send()
            backward_copy(s, b, k).wait_send()


def body(bands, planes, orbitals, plan, cutoff_mask):
    own, slab, size = orbitals.shape[:3]
    steps = plan.shape[0]
    chips = bands // 2
    half = slab // 2 * size
    partners = planes - 1
    vmem = pl.BlockSpec(memory_space=pltpu.VMEM)
    dma = pltpu.SemaphoreType.DMA
    unit = (steps, own)
    out = pl.pallas_call(
        functools.partial(kernel, bands, planes, steps, size, slab),
        out_shape=jax.ShapeDtypeStruct((own, slab * size, size), F32),
        in_specs=[pl.BlockSpec(memory_space=pltpu.SMEM), vmem, vmem, vmem],
        out_specs=vmem,
        scratch_shapes=[
            pltpu.VMEM((slab, size, size), F32),
            pltpu.VMEM((steps, 2 * half, size), F32),
            pltpu.VMEM((steps, half, size), F32),
            pltpu.VMEM((steps, half, size), F32),
            pltpu.VMEM((steps, chips, half // chips, size), F32),
            pltpu.VMEM((steps, 2 * half, size), F32),
            pltpu.VMEM(unit + (slab, size, size), F32),
            pltpu.VMEM(unit + (size, slab, size), F32),
            pltpu.VMEM(unit + (size, slab, size), F32),
            pltpu.VMEM(unit + (slab, size, size), F32),
            dma((steps,)), dma((steps,)),
            dma((steps, chips)), dma((steps, chips)),
            dma((steps, chips)), dma((steps, chips)),
            dma((steps,)), dma((steps,)),
            dma(unit + (partners,)), dma(unit + (partners,)),
            dma(unit + (partners,)), dma(unit + (partners,)),
        ],
        compiler_params=pltpu.CompilerParams(
            collective_id=0, has_side_effects=True, vmem_limit_bytes=40 * 2**20
        ),
    )(
        plan,
        orbitals.reshape(own, slab * size, size),
        cutoff_mask.reshape(size * slab, size),
        jnp.asarray(cas_table(size)),
    )
    return out.reshape(orbitals.shape)


def solution(mesh):
    bands, planes = mesh.shape["band"], mesh.shape["plane"]
    return jax.shard_map(
        functools.partial(body, bands, planes),
        mesh=mesh,
        in_specs=(P("band", "plane", None, None), P(), P(None, "plane", None)),
        out_specs=P("band", "plane", None, None),
        check_vma=False,
    )
```

```python
import functools
import math

import jax
import jax.numpy as jnp
import numpy as np
from jax import lax
from jax.experimental import pallas as pl
from jax.experimental.pallas import tpu as pltpu
from jax.sharding import PartitionSpec as P

MESH = pl.DeviceIdType.MESH
F32 = jnp.float32
BF16 = jnp.bfloat16
OMEGA = 0.106
CORES, Z_LO, RING_X = 2, 4, 4


def cas_table(size):
    index = np.arange(size, dtype=np.int64)
    angle = (index[:, None] * index[None, :] % size) * (2.0 * math.pi / size)
    return (np.cos(angle) + np.sin(angle)).astype(np.float32)


def split(value):
    high = value.astype(BF16)
    low = (value - high.astype(F32)).astype(BF16)
    return high, low


def kernel(
    planes, steps, bands, size, slab, phi_parts, pair_parts,
    plan_hbm, orb_hbm, mask_hbm, table_hbm, out_ref,
    plan_ref, orb_ref, mask_ref, table_ref, filt, cand, crossed, mixed, spread, reduced, summed, phi,
    sent, landed, filtered, returned,
    calm, in_sem, core_send, core_recv, spread_send, spread_recv, z_send, z_recv, up_send, up_recv, gath_send, gath_recv,
    half_send, half_recv,
    fwd_send, fwd_recv, back_send, back_recv,
):
    band = lax.axis_index("band")
    plane = lax.axis_index("plane")
    core = lax.rem(band, CORES)
    z_lo = lax.rem(band // CORES, Z_LO)
    x = band // (CORES * Z_LO)
    rings = planes // 2
    y = plane // 2
    z_hi = lax.rem(plane, 2)
    here = x * CORES + core

    def device(e, z):
        return (e // CORES) * (CORES * Z_LO) + z * CORES + lax.rem(e, CORES)

    order = [(4, 1), (4, 0), (0, 1), (1, 1), (3, 0), (5, 0), (7, 1), (2, 1), (6, 1), (2, 0), (6, 0), (3, 1), (5, 1), (1, 0), (7, 0)]
    partners = [lax.rem(y + far, rings) * 2 + lax.rem(z_hi + other, 2) for far, other in order]
    levels = [lax.rem(z_lo + k, Z_LO) for k in range(1, Z_LO)]

    barrier = pltpu.get_barrier_semaphore()
    greeted = [(device(lax.rem(x + k, RING_X) * CORES + core, z_lo), plane) for k in range(1, RING_X)]
    greeted += [(device(x * CORES + 1 - core, z_lo), plane)]
    greeted += [(device(here, z), plane) for z in levels]
    greeted += [(band, q) for q in partners]
    column = [
        (device(x * CORES + lax.rem(core + k % CORES, CORES), lax.rem(z_lo + k // CORES % Z_LO, Z_LO)),
         2 * y + lax.rem(z_hi + k // (CORES * Z_LO), 2))
        for k in range(1, 2 * CORES * Z_LO)
    ]
    greeted += [column[k - 1] for k in range(1, 2 * CORES * Z_LO) if k % CORES and k != 1 or k > CORES * Z_LO and k % CORES == 0]
    for target in greeted:
        pl.semaphore_signal(barrier, inc=1, device_id=target, device_id_type=MESH)

    loads = [
        pltpu.make_async_copy(source, target, in_sem.at[i])
        for i, (source, target) in enumerate(
            ((plan_hbm, plan_ref), (orb_hbm, orb_ref), (table_hbm, table_ref), (mask_hbm, mask_ref))
        )
    ]
    for load in loads:
        load.start()
    loads[0].wait()
    loads[1].wait()
    for s in range(steps):
        first = (plan_ref[s] == 2 * band).astype(F32)
        second = (plan_ref[s] == 2 * band + 1).astype(F32)
        chosen = orb_ref[0] * first + orb_ref[1] * second
        cand[s] = chosen.reshape(cand.shape[1:])
    loads[2].wait()
    high, low = split(table_ref[...])
    table_left = jnp.concatenate([high, high, low], axis=1)
    table_right = jnp.concatenate([high, high, low], axis=0)

    def times_table(field):
        h, l = split(field)
        return jnp.dot(jnp.concatenate([h, l, h], axis=1), table_right, preferred_element_type=F32)

    def table_times(field):
        h, l = split(field)
        return jnp.dot(table_left, jnp.concatenate([h, l, h], axis=0), preferred_element_type=F32)

    pl.semaphore_wait(barrier, len(greeted))

    def copy(src, dst, send, recv, target):
        return pltpu.make_async_remote_copy(
            src_ref=src, dst_ref=dst, send_sem=send, recv_sem=recv, device_id=target, device_id_type=MESH
        )

    def rows(start, count):
        return pl.ds(pl.multiple_of(start, 8), count)

    def wait_rows(sem, count):
        ref = orb_ref.at[0, pl.ds(0, count)]
        pltpu.make_async_copy(ref, ref, sem).wait()

    piece = size // RING_X
    part = piece // Z_LO
    twin = (device(x * CORES + 1 - core, z_lo), plane)
    own_rows = rows(x * piece, piece)

    def core_copy(s):
        return copy(cand.at[s, :, 1 - core], crossed.at[s], core_send.at[s], core_recv.at[s], twin)

    def mix(s):
        core_copy(s).wait_recv()
        mixed[s] = cand[s, :, core] + crossed[s]

    def spread_out(i):
        s, j0, nj = phi_parts[i]
        js = pl.ds(j0, nj)
        for k in range(1, RING_X):
            to = lax.rem(x + k, RING_X)
            copy(
                mixed.at[s, js, rows(to * piece, piece)], spread.at[s, js, x],
                spread_send.at[i], spread_recv.at[i], (device(to * CORES + core, z_lo), plane),
            ).start()
        spread[s, js, x] = mixed[s, js, own_rows]

    def reduce_z(i):
        s, j0, nj = phi_parts[i]
        js = pl.ds(j0, nj)
        wait_rows(spread_recv.at[i], (RING_X - 1) * nj * piece)
        total = spread[s, js, 0]
        for k in range(1, RING_X):
            total = total + spread[s, js, k]
        reduced[s, js] = total
        for z in levels:
            copy(
                reduced.at[s, js, rows(z * part, part)], summed.at[s, js, z_lo],
                z_send.at[i], z_recv.at[i], (device(here, z), plane),
            ).start()
        summed[s, js, z_lo] = reduced[s, js, rows(z_lo * part, part)]

    def gather_z(i):
        s, j0, nj = phi_parts[i]
        js = pl.ds(j0, nj)
        wait_rows(z_recv.at[i], (Z_LO - 1) * nj * part)
        total = summed[s, js, 0]
        for k in range(1, Z_LO):
            total = total + summed[s, js, k]
        finest = rows(x * piece + z_lo * part, part)
        phi[s, js, core, finest] = total
        for z in levels:
            where = phi.at[s, js, core, finest]
            copy(where, where, up_send.at[i], up_recv.at[i], (device(here, z), plane)).start()

    def gather_x(i):
        s, j0, nj = phi_parts[i]
        js = pl.ds(j0, nj)
        wait_rows(up_recv.at[i], (Z_LO - 1) * nj * part)
        if i == len(phi_parts) - 1:
            for target in column:
                pl.semaphore_signal(calm, inc=1, device_id=target, device_id_type=MESH)
        for k in range(1, RING_X):
            where = phi.at[s, js, core, own_rows]
            to = (device(lax.rem(x + k, RING_X) * CORES + core, z_lo), plane)
            copy(where, where, gath_send.at[i], gath_recv.at[i], to).start()

    def half_copy(i):
        s, j0, nj = phi_parts[i]
        where = phi.at[s, pl.ds(j0, nj), core]
        return copy(where, where, half_send.at[i], half_recv.at[i], twin)

    def gather_core(i):
        wait_rows(gath_recv.at[i], (RING_X - 1) * phi_parts[i][2] * piece)
        half_copy(i).start()

    def all_calm():
        pl.semaphore_wait(calm, len(column))

    def have_phi(i):
        half_copy(i).wait_recv()

    def phi_rows(s, x0, nx):
        return phi[s, pl.ds(x0 // CORES, nx // CORES)].reshape(nx * size, size)

    def wait_blocks(sem, count):
        ref = landed.at[0, 0, pl.ds(0, count)]
        pltpu.make_async_copy(ref, ref, sem).wait()

    own = pl.ds(pl.multiple_of(plane * slab, slab), slab)

    def pair(i):
        s, x0, nx, b0, nb = pair_parts[i]
        for b in range(b0, b0 + nb):
            field = orb_ref[b, pl.ds(x0 * size, nx * size)] * phi_rows(s, x0, nx)
            field = times_table(field)
            field = jnp.concatenate([field[j * size : (j + 1) * size] for j in range(nx)], axis=1)
            field = table_times(field)
            for j in range(nx):
                sent[s, b, x0 + j] = field[:, j * size : (j + 1) * size]
        for b in range(b0, b0 + nb):
            landed[s, b, pl.ds(plane * slab + x0, nx)] = sent[s, b, pl.ds(x0, nx), own]

    def send_pair(i, targets):
        s, x0, nx, b0, nb = pair_parts[i]
        for q in targets:
            copy(
                sent.at[s, pl.ds(b0, nb), pl.ds(x0, nx), pl.ds(pl.multiple_of(q * slab, slab), slab)],
                landed.at[s, pl.ds(b0, nb), pl.ds(plane * slab + x0, nx)],
                fwd_send.at[i], fwd_recv.at[i], (band, q),
            ).start()

    arrived = set()

    def middle(s, b):
        for i, (s1, _, nx, b0, nb) in enumerate(pair_parts):
            if s1 == s and b0 <= b < b0 + nb and i not in arrived:
                arrived.add(i)
                wait_blocks(fwd_recv.at[i], (planes - 1) * nx * nb)
        source = landed.at[s, b].reshape(size * slab, size)
        target = filtered.at[s, b].reshape(size * slab, size)
        field = jnp.concatenate([source[pl.ds(k, size, stride=slab), :] for k in range(slab)], axis=1)
        field = table_times(field) * filt[...]
        field = table_times(field)
        for k in range(slab):
            target[pl.ds(k, size, stride=slab), :] = field[:, k * size : (k + 1) * size]
        for q in partners:
            copy(
                filtered.at[s, b, pl.ds(pl.multiple_of(q * slab, slab), slab)], returned.at[s, b, :, own],
                back_send.at[s, b], back_recv.at[s, b], (band, q),
            ).start()
        returned[s, b, :, own] = filtered[s, b, own]

    def last(s, b):
        wait_blocks(back_recv.at[s, b], (planes - 1) * slab)
        field = table_times(jnp.concatenate([returned[s, b, j] for j in range(slab)], axis=1))
        field = jnp.concatenate([field[:, j * size : (j + 1) * size] for j in range(slab)], axis=0)
        field = times_table(field) * phi_rows(s, 0, slab)
        out_ref[b] = field if s == 0 else out_ref[b] + field

    def screen():
        loads[3].wait()
        row = lax.broadcasted_iota(jnp.int32, (size, size), 0)
        col = lax.broadcasted_iota(jnp.int32, (size, size), 1)

        def wave(index, cell):
            return jnp.where(index < size // 2, index, index - size).astype(F32) * (2.0 * math.pi / cell)

        wave_ac = wave(row, 41.04) ** 2 + wave(col, 20.52) ** 2
        for k in range(slab):
            wave_b = wave(jnp.full((size, size), plane * slab + k, jnp.int32), 41.04)
            squared = wave_ac + wave_b * wave_b
            safe = jnp.where(squared > 0, squared, 1.0)
            screened = -4.0 * math.pi * (1.0 - jnp.exp(-safe / (4.0 * OMEGA * OMEGA))) / safe
            screened = jnp.where(squared > 0, screened, -math.pi / (OMEGA * OMEGA))
            keep = mask_ref[pl.ds(k, size, stride=slab), :].astype(F32)
            filt[:, k * size : (k + 1) * size] = screened * keep * (1.0 / (size * size * size))

    for s in range(steps):
        core_copy(s).start()
    mix(0)
    spread_out(0)
    mix(1)
    spread_out(1)
    screen()
    reduce_z(0)
    gather_z(0)
    reduce_z(1)
    gather_x(0)
    gather_z(1)
    gather_core(0)
    gather_x(1)
    have_phi(0)
    pair(0)
    all_calm()
    send_pair(0, partners)
    pair(1)
    send_pair(1, partners)
    gather_core(1)
    have_phi(1)
    pair(2)
    send_pair(2, partners)
    pair(3)
    send_pair(3, partners)
    units = [(s, b) for s in range(steps) for b in range(bands)]
    for unit in units:
        middle(*unit)
    for s in range(steps):
        core_copy(s).wait_send()
    for i, (_, _, nj) in enumerate(phi_parts):
        wait_rows(spread_send.at[i], (RING_X - 1) * nj * piece)
        wait_rows(z_send.at[i], (Z_LO - 1) * nj * part)
        wait_rows(up_send.at[i], (Z_LO - 1) * nj * part)
        wait_rows(gath_send.at[i], (RING_X - 1) * nj * piece)
        half_copy(i).wait_send()
    for i, (_, _, nx, _, nb) in enumerate(pair_parts):
        wait_blocks(fwd_send.at[i], (planes - 1) * nx * nb)
    for unit in units:
        last(*unit)
    for unit in units:
        wait_blocks(back_send.at[unit], (planes - 1) * slab)


def body(planes, orbitals, plan, cutoff_mask):
    bands, slab, size = orbitals.shape[:3]
    steps = plan.shape[0]
    phi_parts = [(0, 0, 4), (1, 0, 4)]
    pair_parts = [(0, 0, 8, 0, 1), (0, 0, 8, 1, 1), (1, 0, 8, 0, 1), (1, 0, 8, 1, 1)]
    hbm = pl.BlockSpec(memory_space=pltpu.HBM)
    vmem = pltpu.VMEM
    dma = pltpu.SemaphoreType.DMA
    unit = (steps, bands)
    planes_per_core = slab // CORES
    parts, pairs = len(phi_parts), len(pair_parts)
    out = pl.pallas_call(
        functools.partial(kernel, planes, steps, bands, size, slab, phi_parts, pair_parts),
        out_shape=jax.ShapeDtypeStruct((bands, slab * size, size), F32),
        in_specs=[hbm, hbm, hbm, hbm],
        out_specs=pl.BlockSpec(memory_space=vmem),
        scratch_shapes=[
            pltpu.SMEM((steps,), jnp.int32),
            vmem((bands, slab * size, size), F32),
            vmem((size * slab, size), jnp.int32),
            vmem((size, size), F32),
            vmem((size, slab * size), F32),
            vmem((steps, planes_per_core, CORES, size, size), F32),
            vmem((steps, planes_per_core, size, size), F32),
            vmem((steps, planes_per_core, size, size), F32),
            vmem((steps, planes_per_core, RING_X, size // RING_X, size), F32),
            vmem((steps, planes_per_core, size // RING_X, size), F32),
            vmem((steps, planes_per_core, Z_LO, size // RING_X // Z_LO, size), F32),
            vmem((steps, planes_per_core, CORES, size, size), F32),
            vmem(unit + (slab, size, size), F32),
            vmem(unit + (size, slab, size), F32),
            vmem(unit + (size, slab, size), F32),
            vmem(unit + (slab, size, size), F32),
            pltpu.SemaphoreType.REGULAR,
            dma((4,)), dma((steps,)), dma((steps,)),
            *(dma((parts,)) for _ in range(10)),
            dma((pairs,)), dma((pairs,)),
            dma(unit), dma(unit),
        ],
        compiler_params=pltpu.CompilerParams(
            collective_id=0, has_side_effects=True, vmem_limit_bytes=40 * 2**20
        ),
    )(
        *(
            pltpu.with_memory_space_constraint(value, pltpu.HBM)
            for value in (
                plan,
                orbitals.reshape(bands, slab * size, size),
                cutoff_mask.reshape(size * slab, size),
                jnp.asarray(cas_table(size)),
            )
        )
    )
    return out.reshape(orbitals.shape)


def solution(mesh):
    return jax.shard_map(
        functools.partial(body, mesh.shape["plane"]),
        mesh=mesh,
        in_specs=(P("band", "plane", None, None), P(), P(None, "plane", None)),
        out_specs=P("band", "plane", None, None),
        check_vma=False,
    )
```

```python
import functools
import math

import jax
import jax.numpy as jnp
import numpy as np
from jax import lax
from jax.experimental import pallas as pl
from jax.experimental.pallas import tpu as pltpu
from jax.sharding import PartitionSpec as P

MESH = pl.DeviceIdType.MESH
F32 = jnp.float32
BF16 = jnp.bfloat16
OMEGA = 0.106
CORES, Z_LO, RING_X = 2, 4, 4


def cas_table(size):
    index = np.arange(size, dtype=np.int64)
    angle = (index[:, None] * index[None, :] % size) * (2.0 * math.pi / size)
    return (np.cos(angle) + np.sin(angle)).astype(np.float32)


def split(value):
    high = value.astype(BF16)
    low = (value - high.astype(F32)).astype(BF16)
    return high, low


def kernel(
    planes, steps, bands, size, slab, phi_parts, pair_parts,
    plan_hbm, orb_hbm, mask_hbm, table_hbm, out_ref,
    plan_ref, orb_ref, mask_ref, table_ref, filt, cand, crossed, mixed, spread, reduced, summed, phi,
    sent, landed, filtered, returned,
    calm, in_sem, core_send, core_recv, spread_send, spread_recv, z_send, z_recv, up_send, up_recv, gath_send, gath_recv,
    half_send, half_recv,
    fwd_send, fwd_recv, back_send, back_recv,
):
    band = lax.axis_index("band")
    plane = lax.axis_index("plane")
    core = lax.rem(band, CORES)
    z_lo = lax.rem(band // CORES, Z_LO)
    x = band // (CORES * Z_LO)
    rings = planes // 2
    y = plane // 2
    z_hi = lax.rem(plane, 2)
    here = x * CORES + core

    def device(e, z):
        return (e // CORES) * (CORES * Z_LO) + z * CORES + lax.rem(e, CORES)

    order = [(4, 1), (4, 0), (0, 1), (1, 1), (3, 0), (5, 0), (7, 1), (2, 1), (6, 1), (2, 0), (6, 0), (3, 1), (5, 1), (1, 0), (7, 0)]
    partners = [lax.rem(y + far, rings) * 2 + lax.rem(z_hi + other, 2) for far, other in order]
    levels = [lax.rem(z_lo + k, Z_LO) for k in range(1, Z_LO)]

    loads = [
        pltpu.make_async_copy(source, target, in_sem.at[i])
        for i, (source, target) in enumerate(
            ((plan_hbm, plan_ref), (orb_hbm, orb_ref), (table_hbm, table_ref), (mask_hbm, mask_ref))
        )
    ]
    for load in loads:
        load.start()

    barrier = pltpu.get_barrier_semaphore()
    greeted = [(device(lax.rem(x + k, RING_X) * CORES + core, z_lo), plane) for k in range(1, RING_X)]
    greeted += [(device(x * CORES + 1 - core, z_lo), plane)]
    greeted += [(device(here, z), plane) for z in levels]
    greeted += [(band, q) for q in partners]
    column = [
        (device(x * CORES + lax.rem(core + k % CORES, CORES), lax.rem(z_lo + k // CORES % Z_LO, Z_LO)),
         2 * y + lax.rem(z_hi + k // (CORES * Z_LO), 2))
        for k in range(1, 2 * CORES * Z_LO)
    ]
    greeted += [column[k - 1] for k in range(1, 2 * CORES * Z_LO) if k % CORES and k != 1 or k > CORES * Z_LO and k % CORES == 0]
    for target in greeted:
        pl.semaphore_signal(barrier, inc=1, device_id=target, device_id_type=MESH)

    loads[0].wait()
    loads[1].wait()
    def times_table(field):
        high, low = split(table_ref[...])
        table_right = jnp.concatenate([high, high, low], axis=0)
        h, l = split(field)
        return jnp.dot(jnp.concatenate([h, l, h], axis=1), table_right, preferred_element_type=F32)

    def table_times(field):
        high, low = split(table_ref[...])
        table_left = jnp.concatenate([high, high, low], axis=1)
        h, l = split(field)
        return jnp.dot(table_left, jnp.concatenate([h, l, h], axis=0), preferred_element_type=F32)

    def candidate(s):
        first = (plan_ref[s] == 2 * band).astype(F32)
        second = (plan_ref[s] == 2 * band + 1).astype(F32)
        chosen = orb_ref[0] * first + orb_ref[1] * second
        cand[s] = chosen.reshape(cand.shape[1:])

    candidate(0)
    pl.semaphore_wait(barrier, len(greeted))

    def copy(src, dst, send, recv, target):
        return pltpu.make_async_remote_copy(
            src_ref=src, dst_ref=dst, send_sem=send, recv_sem=recv, device_id=target, device_id_type=MESH
        )

    def rows(start, count):
        return pl.ds(pl.multiple_of(start, 8), count)

    def wait_rows(sem, count):
        ref = orb_ref.at[0, pl.ds(0, count)]
        pltpu.make_async_copy(ref, ref, sem).wait()

    piece = size // RING_X
    part = piece // Z_LO
    twin = (device(x * CORES + 1 - core, z_lo), plane)
    own_rows = rows(x * piece, piece)

    def core_copy(s):
        return copy(cand.at[s, :, 1 - core], crossed.at[s], core_send.at[s], core_recv.at[s], twin)

    def mix(s):
        core_copy(s).wait_recv()
        mixed[s] = cand[s, :, core] + crossed[s]

    def spread_out(i):
        s, j0, nj = phi_parts[i]
        js = pl.ds(j0, nj)
        for k in range(1, RING_X):
            to = lax.rem(x + k, RING_X)
            copy(
                mixed.at[s, js, rows(to * piece, piece)], spread.at[s, js, x],
                spread_send.at[i], spread_recv.at[i], (device(to * CORES + core, z_lo), plane),
            ).start()
        spread[s, js, x] = mixed[s, js, own_rows]

    def reduce_z(i):
        s, j0, nj = phi_parts[i]
        js = pl.ds(j0, nj)
        wait_rows(spread_recv.at[i], (RING_X - 1) * nj * piece)
        total = spread[s, js, 0]
        for k in range(1, RING_X):
            total = total + spread[s, js, k]
        reduced[s, js] = total
        for z in levels:
            copy(
                reduced.at[s, js, rows(z * part, part)], summed.at[s, js, z_lo],
                z_send.at[i], z_recv.at[i], (device(here, z), plane),
            ).start()
        summed[s, js, z_lo] = reduced[s, js, rows(z_lo * part, part)]

    def gather_z(i):
        s, j0, nj = phi_parts[i]
        js = pl.ds(j0, nj)
        wait_rows(z_recv.at[i], (Z_LO - 1) * nj * part)
        total = summed[s, js, 0]
        for k in range(1, Z_LO):
            total = total + summed[s, js, k]
        finest = rows(x * piece + z_lo * part, part)
        phi[s, js, core, finest] = total
        for z in levels:
            where = phi.at[s, js, core, finest]
            copy(where, where, up_send.at[i], up_recv.at[i], (device(here, z), plane)).start()

    def gather_x(i):
        s, j0, nj = phi_parts[i]
        js = pl.ds(j0, nj)
        wait_rows(up_recv.at[i], (Z_LO - 1) * nj * part)
        if i == len(phi_parts) - 1:
            for target in column:
                pl.semaphore_signal(calm, inc=1, device_id=target, device_id_type=MESH)
        for k in range(1, RING_X):
            where = phi.at[s, js, core, own_rows]
            to = (device(lax.rem(x + k, RING_X) * CORES + core, z_lo), plane)
            copy(where, where, gath_send.at[i], gath_recv.at[i], to).start()

    def half_copy(i):
        s, j0, nj = phi_parts[i]
        where = phi.at[s, pl.ds(j0, nj), core]
        return copy(where, where, half_send.at[i], half_recv.at[i], twin)

    def gather_core(i):
        wait_rows(gath_recv.at[i], (RING_X - 1) * phi_parts[i][2] * piece)
        half_copy(i).start()

    def all_calm():
        pl.semaphore_wait(calm, len(column))

    def have_phi(i):
        half_copy(i).wait_recv()

    def phi_rows(s, x0, nx):
        return phi[s, pl.ds(x0 // CORES, nx // CORES)].reshape(nx * size, size)

    def wait_blocks(sem, count):
        ref = landed.at[0, 0, pl.ds(0, count)]
        pltpu.make_async_copy(ref, ref, sem).wait()

    own = pl.ds(pl.multiple_of(plane * slab, slab), slab)

    def pair(i):
        s, x0, nx, b0, nb = pair_parts[i]
        for b in range(b0, b0 + nb):
            field = orb_ref[b, pl.ds(x0 * size, nx * size)] * phi_rows(s, x0, nx)
            field = times_table(field)
            field = jnp.concatenate([field[j * size : (j + 1) * size] for j in range(nx)], axis=1)
            field = table_times(field)
            for j in range(nx):
                sent[s, b, x0 + j] = field[:, j * size : (j + 1) * size]
        for b in range(b0, b0 + nb):
            landed[s, b, pl.ds(plane * slab + x0, nx)] = sent[s, b, pl.ds(x0, nx), own]

    def send_pair(i, targets):
        s, x0, nx, b0, nb = pair_parts[i]
        for q in targets:
            copy(
                sent.at[s, pl.ds(b0, nb), pl.ds(x0, nx), pl.ds(pl.multiple_of(q * slab, slab), slab)],
                landed.at[s, pl.ds(b0, nb), pl.ds(plane * slab + x0, nx)],
                fwd_send.at[i], fwd_recv.at[i], (band, q),
            ).start()

    arrived = set()

    def middle(s, b):
        for i, (s1, _, nx, b0, nb) in enumerate(pair_parts):
            if s1 == s and b0 <= b < b0 + nb and i not in arrived:
                arrived.add(i)
                wait_blocks(fwd_recv.at[i], (planes - 1) * nx * nb)
        source = landed.at[s, b].reshape(size * slab, size)
        target = filtered.at[s, b].reshape(size * slab, size)
        field = jnp.concatenate([source[pl.ds(k, size, stride=slab), :] for k in range(slab)], axis=1)
        field = table_times(field) * filt[...]
        field = table_times(field)
        for k in range(slab):
            target[pl.ds(k, size, stride=slab), :] = field[:, k * size : (k + 1) * size]
        r = (0, 3, 7, 11)[s * bands + b]
        for q in partners[r:] + partners[:r]:
            copy(
                filtered.at[s, b, pl.ds(pl.multiple_of(q * slab, slab), slab)], returned.at[s, b, :, own],
                back_send.at[s, b], back_recv.at[s, b], (band, q),
            ).start()
        returned[s, b, :, own] = filtered[s, b, own]

    def last(s, b):
        wait_blocks(back_recv.at[s, b], (planes - 1) * slab)
        field = table_times(jnp.concatenate([returned[s, b, j] for j in range(slab)], axis=1))
        field = jnp.concatenate([field[:, j * size : (j + 1) * size] for j in range(slab)], axis=0)
        field = times_table(field) * phi_rows(s, 0, slab)
        out_ref[b] = field if s == 0 else out_ref[b] + field

    def screen():
        loads[2].wait()
        loads[3].wait()
        row = lax.broadcasted_iota(jnp.int32, (size, size), 0)
        col = lax.broadcasted_iota(jnp.int32, (size, size), 1)

        def wave(index, cell):
            return jnp.where(index < size // 2, index, index - size).astype(F32) * (2.0 * math.pi / cell)

        wave_ac = wave(row, 41.04) ** 2 + wave(col, 20.52) ** 2
        for k in range(slab):
            wave_b = wave(jnp.full((size, size), plane * slab + k, jnp.int32), 41.04)
            squared = wave_ac + wave_b * wave_b
            safe = jnp.where(squared > 0, squared, 1.0)
            screened = -4.0 * math.pi * (1.0 - jnp.exp(-safe / (4.0 * OMEGA * OMEGA))) / safe
            screened = jnp.where(squared > 0, screened, -math.pi / (OMEGA * OMEGA))
            keep = mask_ref[pl.ds(k, size, stride=slab), :].astype(F32)
            filt[:, k * size : (k + 1) * size] = screened * keep * (1.0 / (size * size * size))

    core_copy(0).start()
    candidate(1)
    core_copy(1).start()
    mix(0)
    spread_out(0)
    spread_out(1)
    mix(1)
    spread_out(2)
    screen()
    reduce_z(0)
    reduce_z(1)
    reduce_z(2)
    gather_z(0)
    gather_z(1)
    gather_z(2)
    gather_x(0)
    gather_x(1)
    gather_x(2)
    gather_core(0)
    gather_core(1)
    have_phi(0)
    have_phi(1)
    pair(0)
    all_calm()
    send_pair(0, partners)
    pair(1)
    send_pair(1, partners[3:] + partners[:3])
    gather_core(2)
    have_phi(2)
    pair(2)
    send_pair(2, partners[7:] + partners[:7])
    pair(3)
    send_pair(3, partners[11:] + partners[:11])
    units = [(s, b) for s in range(steps) for b in range(bands)]
    for unit in units:
        middle(*unit)
    for s in range(steps):
        core_copy(s).wait_send()
    for i, (_, _, nj) in enumerate(phi_parts):
        wait_rows(spread_send.at[i], (RING_X - 1) * nj * piece)
        wait_rows(z_send.at[i], (Z_LO - 1) * nj * part)
        wait_rows(up_send.at[i], (Z_LO - 1) * nj * part)
        wait_rows(gath_send.at[i], (RING_X - 1) * nj * piece)
        half_copy(i).wait_send()
    for i, (_, _, nx, _, nb) in enumerate(pair_parts):
        wait_blocks(fwd_send.at[i], (planes - 1) * nx * nb)
    for unit in units:
        last(*unit)
    for unit in units:
        wait_blocks(back_send.at[unit], (planes - 1) * slab)


def body(planes, orbitals, plan, cutoff_mask):
    bands, slab, size = orbitals.shape[:3]
    steps = plan.shape[0]
    phi_parts = [(0, 0, 2), (0, 2, 2), (1, 0, 4)]
    pair_parts = [(0, 0, 8, 0, 1), (0, 0, 8, 1, 1), (1, 0, 8, 0, 1), (1, 0, 8, 1, 1)]
    hbm = pl.BlockSpec(memory_space=pltpu.HBM)
    vmem = pltpu.VMEM
    dma = pltpu.SemaphoreType.DMA
    unit = (steps, bands)
    planes_per_core = slab // CORES
    parts, pairs = len(phi_parts), len(pair_parts)
    out = pl.pallas_call(
        functools.partial(kernel, planes, steps, bands, size, slab, phi_parts, pair_parts),
        out_shape=jax.ShapeDtypeStruct((bands, slab * size, size), F32),
        in_specs=[hbm, hbm, hbm, hbm],
        out_specs=pl.BlockSpec(memory_space=vmem),
        scratch_shapes=[
            pltpu.SMEM((steps,), jnp.int32),
            vmem((bands, slab * size, size), F32),
            vmem((size * slab, size), jnp.int32),
            vmem((size, size), F32),
            vmem((size, slab * size), F32),
            vmem((steps, planes_per_core, CORES, size, size), F32),
            vmem((steps, planes_per_core, size, size), F32),
            vmem((steps, planes_per_core, size, size), F32),
            vmem((steps, planes_per_core, RING_X, size // RING_X, size), F32),
            vmem((steps, planes_per_core, size // RING_X, size), F32),
            vmem((steps, planes_per_core, Z_LO, size // RING_X // Z_LO, size), F32),
            vmem((steps, planes_per_core, CORES, size, size), F32),
            vmem(unit + (slab, size, size), F32),
            vmem(unit + (size, slab, size), F32),
            vmem(unit + (size, slab, size), F32),
            vmem(unit + (slab, size, size), F32),
            pltpu.SemaphoreType.REGULAR,
            dma((4,)), dma((steps,)), dma((steps,)),
            *(dma((parts,)) for _ in range(10)),
            dma((pairs,)), dma((pairs,)),
            dma(unit), dma(unit),
        ],
        compiler_params=pltpu.CompilerParams(
            collective_id=0, has_side_effects=True, vmem_limit_bytes=40 * 2**20
        ),
    )(
        *(
            pltpu.with_memory_space_constraint(value, pltpu.HBM)
            for value in (
                plan,
                orbitals.reshape(bands, slab * size, size),
                cutoff_mask.reshape(size * slab, size),
                jnp.asarray(cas_table(size)),
            )
        )
    )
    return out.reshape(orbitals.shape)


def solution(mesh):
    return jax.shard_map(
        functools.partial(body, mesh.shape["plane"]),
        mesh=mesh,
        in_specs=(P("band", "plane", None, None), P(), P(None, "plane", None)),
        out_specs=P("band", "plane", None, None),
        check_vma=False,
    )
```

```python
import functools
import math

import jax
import jax.numpy as jnp
import numpy as np
from jax import lax
from jax.experimental import pallas as pl
from jax.experimental.pallas import tpu as pltpu
from jax.sharding import PartitionSpec as P

MESH = pl.DeviceIdType.MESH
F32 = jnp.float32
BF16 = jnp.bfloat16
OMEGA = 0.106
CORES, Z_LO, RING_X = 2, 4, 4


def cas_table(size):
    index = np.arange(size, dtype=np.int64)
    angle = (index[:, None] * index[None, :] % size) * (2.0 * math.pi / size)
    return (np.cos(angle) + np.sin(angle)).astype(np.float32)


def split(value):
    high = value.astype(BF16)
    rest = value - high.astype(F32)
    middle = rest.astype(BF16)
    return high, middle, (rest - middle.astype(F32)).astype(BF16)


def terms(value, first, exact):
    h, m, l = split(value)
    if not exact:
        return (h, h, m) if first else (h, m, h)
    return (h, h, m, m, h, l) if first else (h, m, h, m, l, h)


def kernel(
    planes, steps, bands, size, slab, phi_parts, pair_parts,
    plan_hbm, orb_hbm, mask_hbm, table_hbm, out_ref,
    plan_ref, orb_ref, mask_ref, table_ref, filt, cand, crossed, mixed, spread, reduced, summed, phi,
    sent, landed, filtered, returned,
    calm, in_sem, core_send, core_recv, spread_send, spread_recv, z_send, z_recv, up_send, up_recv, gath_send, gath_recv,
    half_send, half_recv,
    fwd_send, fwd_recv, back_send, back_recv,
):
    band = lax.axis_index("band")
    plane = lax.axis_index("plane")
    core = lax.rem(band, CORES)
    z_lo = lax.rem(band // CORES, Z_LO)
    x = band // (CORES * Z_LO)
    rings = planes // 2
    y = plane // 2
    z_hi = lax.rem(plane, 2)
    here = x * CORES + core

    def device(e, z):
        return (e // CORES) * (CORES * Z_LO) + z * CORES + lax.rem(e, CORES)

    order = [(4, 1), (4, 0), (0, 1), (1, 1), (3, 0), (5, 0), (7, 1), (2, 1), (6, 1), (2, 0), (6, 0), (3, 1), (5, 1), (1, 0), (7, 0)]
    partners = [lax.rem(y + far, rings) * 2 + lax.rem(z_hi + other, 2) for far, other in order]
    levels = [lax.rem(z_lo + k, Z_LO) for k in range(1, Z_LO)]

    loads = [
        pltpu.make_async_copy(source, target, in_sem.at[i])
        for i, (source, target) in enumerate(
            ((plan_hbm, plan_ref), (orb_hbm, orb_ref), (table_hbm, table_ref), (mask_hbm, mask_ref))
        )
    ]
    for load in loads:
        load.start()

    barrier = pltpu.get_barrier_semaphore()
    greeted = [(device(lax.rem(x + k, RING_X) * CORES + core, z_lo), plane) for k in range(1, RING_X)]
    greeted += [(device(x * CORES + 1 - core, z_lo), plane)]
    greeted += [(device(here, z), plane) for z in levels]
    greeted += [(band, q) for q in partners]
    column = [
        (device(x * CORES + lax.rem(core + k % CORES, CORES), lax.rem(z_lo + k // CORES % Z_LO, Z_LO)),
         2 * y + lax.rem(z_hi + k // (CORES * Z_LO), 2))
        for k in range(1, 2 * CORES * Z_LO)
    ]
    greeted += [column[k - 1] for k in range(1, 2 * CORES * Z_LO) if k % CORES and k != 1 or k > CORES * Z_LO and k % CORES == 0]
    for target in greeted:
        pl.semaphore_signal(barrier, inc=1, device_id=target, device_id_type=MESH)

    loads[0].wait()
    loads[1].wait()
    def times_table(field, exact=False):
        left = jnp.concatenate(terms(field, False, exact), axis=1)
        right = jnp.concatenate(terms(table_ref[...], True, exact), axis=0)
        return jnp.dot(left, right, preferred_element_type=F32)

    def table_times(field, exact=False):
        left = jnp.concatenate(terms(table_ref[...], True, exact), axis=1)
        right = jnp.concatenate(terms(field, False, exact), axis=0)
        return jnp.dot(left, right, preferred_element_type=F32)

    def candidate(s):
        first = (plan_ref[s] == 2 * band).astype(F32)
        second = (plan_ref[s] == 2 * band + 1).astype(F32)
        chosen = orb_ref[0] * first + orb_ref[1] * second
        cand[s] = chosen.reshape(cand.shape[1:])

    candidate(0)
    pl.semaphore_wait(barrier, len(greeted))

    def copy(src, dst, send, recv, target):
        return pltpu.make_async_remote_copy(
            src_ref=src, dst_ref=dst, send_sem=send, recv_sem=recv, device_id=target, device_id_type=MESH
        )

    def rows(start, count):
        return pl.ds(pl.multiple_of(start, 8), count)

    def wait_rows(sem, count):
        ref = orb_ref.at[0, pl.ds(0, count)]
        pltpu.make_async_copy(ref, ref, sem).wait()

    piece = size // RING_X
    part = piece // Z_LO
    twin = (device(x * CORES + 1 - core, z_lo), plane)
    own_rows = rows(x * piece, piece)

    def core_copy(s):
        return copy(cand.at[s, :, 1 - core], crossed.at[s], core_send.at[s], core_recv.at[s], twin)

    def mix(s):
        core_copy(s).wait_recv()
        mixed[s] = cand[s, :, core] + crossed[s]

    def spread_out(i):
        s, j0, nj = phi_parts[i]
        js = pl.ds(j0, nj)
        for k in range(1, RING_X):
            to = lax.rem(x + k, RING_X)
            copy(
                mixed.at[s, js, rows(to * piece, piece)], spread.at[s, js, x],
                spread_send.at[i], spread_recv.at[i], (device(to * CORES + core, z_lo), plane),
            ).start()
        spread[s, js, x] = mixed[s, js, own_rows]

    def reduce_z(i):
        s, j0, nj = phi_parts[i]
        js = pl.ds(j0, nj)
        wait_rows(spread_recv.at[i], (RING_X - 1) * nj * piece)
        total = spread[s, js, 0]
        for k in range(1, RING_X):
            total = total + spread[s, js, k]
        reduced[s, js] = total
        for z in levels:
            copy(
                reduced.at[s, js, rows(z * part, part)], summed.at[s, js, z_lo],
                z_send.at[i], z_recv.at[i], (device(here, z), plane),
            ).start()
        summed[s, js, z_lo] = reduced[s, js, rows(z_lo * part, part)]

    def gather_z(i):
        s, j0, nj = phi_parts[i]
        js = pl.ds(j0, nj)
        wait_rows(z_recv.at[i], (Z_LO - 1) * nj * part)
        total = summed[s, js, 0]
        for k in range(1, Z_LO):
            total = total + summed[s, js, k]
        finest = rows(x * piece + z_lo * part, part)
        phi[s, js, core, finest] = total
        for z in levels:
            where = phi.at[s, js, core, finest]
            copy(where, where, up_send.at[i], up_recv.at[i], (device(here, z), plane)).start()

    def gather_x(i):
        s, j0, nj = phi_parts[i]
        js = pl.ds(j0, nj)
        wait_rows(up_recv.at[i], (Z_LO - 1) * nj * part)
        if i == len(phi_parts) - 1:
            for target in column:
                pl.semaphore_signal(calm, inc=1, device_id=target, device_id_type=MESH)
        for k in range(1, RING_X):
            where = phi.at[s, js, core, own_rows]
            to = (device(lax.rem(x + k, RING_X) * CORES + core, z_lo), plane)
            copy(where, where, gath_send.at[i], gath_recv.at[i], to).start()

    def half_copy(i):
        s, j0, nj = phi_parts[i]
        where = phi.at[s, pl.ds(j0, nj), core]
        return copy(where, where, half_send.at[i], half_recv.at[i], twin)

    def gather_core(i):
        wait_rows(gath_recv.at[i], (RING_X - 1) * phi_parts[i][2] * piece)
        half_copy(i).start()

    def all_calm():
        pl.semaphore_wait(calm, len(column))

    def have_phi(i):
        half_copy(i).wait_recv()

    def phi_rows(s, x0, nx):
        return phi[s, pl.ds(x0 // CORES, nx // CORES)].reshape(nx * size, size)

    def wait_blocks(sem, count):
        ref = landed.at[0, 0, pl.ds(0, count)]
        pltpu.make_async_copy(ref, ref, sem).wait()

    own = pl.ds(pl.multiple_of(plane * slab, slab), slab)

    def pair(i):
        s, x0, nx, b0, nb = pair_parts[i]
        for b in range(b0, b0 + nb):
            field = orb_ref[b, pl.ds(x0 * size, nx * size)] * phi_rows(s, x0, nx)
            field = times_table(field, exact=True)
            field = jnp.concatenate([field[j * size : (j + 1) * size] for j in range(nx)], axis=1)
            field = table_times(field, exact=True)
            for j in range(nx):
                sent[s, b, x0 + j] = field[:, j * size : (j + 1) * size]
        for b in range(b0, b0 + nb):
            landed[s, b, pl.ds(plane * slab + x0, nx)] = sent[s, b, pl.ds(x0, nx), own]

    def send_pair(i, targets):
        s, x0, nx, b0, nb = pair_parts[i]
        for q in targets:
            copy(
                sent.at[s, pl.ds(b0, nb), pl.ds(x0, nx), pl.ds(pl.multiple_of(q * slab, slab), slab)],
                landed.at[s, pl.ds(b0, nb), pl.ds(plane * slab + x0, nx)],
                fwd_send.at[i], fwd_recv.at[i], (band, q),
            ).start()

    arrived = set()

    def middle(s, b):
        for i, (s1, _, nx, b0, nb) in enumerate(pair_parts):
            if s1 == s and b0 <= b < b0 + nb and i not in arrived:
                arrived.add(i)
                wait_blocks(fwd_recv.at[i], (planes - 1) * nx * nb)
        source = landed.at[s, b].reshape(size * slab, size)
        target = filtered.at[s, b].reshape(size * slab, size)
        field = jnp.concatenate([source[pl.ds(k, size, stride=slab), :] for k in range(slab)], axis=1)
        field = table_times(field, exact=True) * filt[...]
        field = table_times(field)
        for k in range(slab):
            target[pl.ds(k, size, stride=slab), :] = field[:, k * size : (k + 1) * size]
        r = (0, 3, 7, 11)[s * bands + b]
        for q in partners[r:] + partners[:r]:
            copy(
                filtered.at[s, b, pl.ds(pl.multiple_of(q * slab, slab), slab)], returned.at[s, b, :, own],
                back_send.at[s, b], back_recv.at[s, b], (band, q),
            ).start()
        returned[s, b, :, own] = filtered[s, b, own]

    def last(s, b):
        wait_blocks(back_recv.at[s, b], (planes - 1) * slab)
        field = table_times(jnp.concatenate([returned[s, b, j] for j in range(slab)], axis=1))
        field = jnp.concatenate([field[:, j * size : (j + 1) * size] for j in range(slab)], axis=0)
        field = times_table(field) * phi_rows(s, 0, slab)
        out_ref[b] = field if s == 0 else out_ref[b] + field

    def screen():
        loads[2].wait()
        loads[3].wait()
        row = lax.broadcasted_iota(jnp.int32, (size, size), 0)
        col = lax.broadcasted_iota(jnp.int32, (size, size), 1)

        def wave(index, cell):
            return jnp.where(index < size // 2, index, index - size).astype(F32) * (2.0 * math.pi / cell)

        wave_ac = wave(row, 41.04) ** 2 + wave(col, 20.52) ** 2
        for k in range(slab):
            wave_b = wave(jnp.full((size, size), plane * slab + k, jnp.int32), 41.04)
            squared = wave_ac + wave_b * wave_b
            safe = jnp.where(squared > 0, squared, 1.0)
            screened = -4.0 * math.pi * (1.0 - jnp.exp(-safe / (4.0 * OMEGA * OMEGA))) / safe
            screened = jnp.where(squared > 0, screened, -math.pi / (OMEGA * OMEGA))
            keep = mask_ref[pl.ds(k, size, stride=slab), :].astype(F32)
            filt[:, k * size : (k + 1) * size] = screened * keep * (1.0 / (size * size * size))

    core_copy(0).start()
    candidate(1)
    core_copy(1).start()
    mix(0)
    spread_out(0)
    spread_out(1)
    mix(1)
    spread_out(2)
    screen()
    reduce_z(0)
    reduce_z(1)
    reduce_z(2)
    gather_z(0)
    gather_z(1)
    gather_z(2)
    gather_x(0)
    gather_x(1)
    gather_x(2)
    gather_core(0)
    gather_core(1)
    have_phi(0)
    have_phi(1)
    pair(0)
    all_calm()
    send_pair(0, partners)
    pair(1)
    send_pair(1, partners[3:] + partners[:3])
    gather_core(2)
    have_phi(2)
    pair(2)
    send_pair(2, partners[7:] + partners[:7])
    pair(3)
    send_pair(3, partners[11:] + partners[:11])
    units = [(s, b) for s in range(steps) for b in range(bands)]
    for unit in units:
        middle(*unit)
    for s in range(steps):
        core_copy(s).wait_send()
    for i, (_, _, nj) in enumerate(phi_parts):
        wait_rows(spread_send.at[i], (RING_X - 1) * nj * piece)
        wait_rows(z_send.at[i], (Z_LO - 1) * nj * part)
        wait_rows(up_send.at[i], (Z_LO - 1) * nj * part)
        wait_rows(gath_send.at[i], (RING_X - 1) * nj * piece)
        half_copy(i).wait_send()
    for i, (_, _, nx, _, nb) in enumerate(pair_parts):
        wait_blocks(fwd_send.at[i], (planes - 1) * nx * nb)
    for unit in units:
        last(*unit)
    for unit in units:
        wait_blocks(back_send.at[unit], (planes - 1) * slab)


def body(planes, orbitals, plan, cutoff_mask):
    bands, slab, size = orbitals.shape[:3]
    steps = plan.shape[0]
    phi_parts = [(0, 0, 2), (0, 2, 2), (1, 0, 4)]
    pair_parts = [(0, 0, 8, 0, 1), (0, 0, 8, 1, 1), (1, 0, 8, 0, 1), (1, 0, 8, 1, 1)]
    hbm = pl.BlockSpec(memory_space=pltpu.HBM)
    vmem = pltpu.VMEM
    dma = pltpu.SemaphoreType.DMA
    unit = (steps, bands)
    planes_per_core = slab // CORES
    parts, pairs = len(phi_parts), len(pair_parts)
    out = pl.pallas_call(
        functools.partial(kernel, planes, steps, bands, size, slab, phi_parts, pair_parts),
        out_shape=jax.ShapeDtypeStruct((bands, slab * size, size), F32),
        in_specs=[hbm, hbm, hbm, hbm],
        out_specs=pl.BlockSpec(memory_space=vmem),
        scratch_shapes=[
            pltpu.SMEM((steps,), jnp.int32),
            vmem((bands, slab * size, size), F32),
            vmem((size * slab, size), jnp.int32),
            vmem((size, size), F32),
            vmem((size, slab * size), F32),
            vmem((steps, planes_per_core, CORES, size, size), F32),
            vmem((steps, planes_per_core, size, size), F32),
            vmem((steps, planes_per_core, size, size), F32),
            vmem((steps, planes_per_core, RING_X, size // RING_X, size), F32),
            vmem((steps, planes_per_core, size // RING_X, size), F32),
            vmem((steps, planes_per_core, Z_LO, size // RING_X // Z_LO, size), F32),
            vmem((steps, planes_per_core, CORES, size, size), F32),
            vmem(unit + (slab, size, size), F32),
            vmem(unit + (size, slab, size), F32),
            vmem(unit + (size, slab, size), F32),
            vmem(unit + (slab, size, size), F32),
            pltpu.SemaphoreType.REGULAR,
            dma((4,)), dma((steps,)), dma((steps,)),
            *(dma((parts,)) for _ in range(10)),
            dma((pairs,)), dma((pairs,)),
            dma(unit), dma(unit),
        ],
        compiler_params=pltpu.CompilerParams(
            collective_id=0, has_side_effects=True, vmem_limit_bytes=40 * 2**20
        ),
    )(
        *(
            pltpu.with_memory_space_constraint(value, pltpu.HBM)
            for value in (
                plan,
                orbitals.reshape(bands, slab * size, size),
                cutoff_mask.reshape(size * slab, size),
                jnp.asarray(cas_table(size)),
            )
        )
    )
    return out.reshape(orbitals.shape)


def solution(mesh):
    return jax.shard_map(
        functools.partial(body, mesh.shape["plane"]),
        mesh=mesh,
        in_specs=(P("band", "plane", None, None), P(), P(None, "plane", None)),
        out_specs=P("band", "plane", None, None),
        check_vma=False,
    )
```

```python
import functools
import math

import jax
import jax.numpy as jnp
import numpy as np
from jax import lax
from jax.experimental import pallas as pl
from jax.experimental.pallas import tpu as pltpu
from jax.sharding import PartitionSpec as P

MESH = pl.DeviceIdType.MESH
F32 = jnp.float32
BF16 = jnp.bfloat16
OMEGA = 0.106
CORES, Z_LO, RING_X = 2, 4, 4


def cas_table(size):
    index = np.arange(size, dtype=np.int64)
    angle = (index[:, None] * index[None, :] % size) * (2.0 * math.pi / size)
    return (np.cos(angle) + np.sin(angle)).astype(np.float32)


def split(value):
    high = value.astype(BF16)
    rest = value - high.astype(F32)
    middle = rest.astype(BF16)
    return high, middle, (rest - middle.astype(F32)).astype(BF16)


def terms(value, first, exact):
    h, m, l = split(value)
    if not exact:
        return (h, h, m) if first else (h, m, h)
    return (h, h, m, m, h, l) if first else (h, m, h, m, l, h)


def kernel(
    planes, steps, bands, size, slab, phi_parts, pair_parts,
    plan_hbm, orb_hbm, mask_hbm, table_hbm, out_ref,
    plan_ref, orb_ref, mask_ref, table_ref, filt, cand, crossed, mixed, spread, reduced, summed, phi,
    sent, landed, filtered, returned,
    calm, in_sem, core_send, core_recv, spread_send, spread_recv, z_send, z_recv, up_send, up_recv, gath_send, gath_recv,
    half_send, half_recv,
    fwd_send, fwd_recv, back_send, back_recv,
):
    band = lax.axis_index("band")
    plane = lax.axis_index("plane")
    core = lax.rem(band, CORES)
    z_lo = lax.rem(band // CORES, Z_LO)
    x = band // (CORES * Z_LO)
    rings = planes // 2
    y = plane // 2
    z_hi = lax.rem(plane, 2)
    here = x * CORES + core

    def device(e, z):
        return (e // CORES) * (CORES * Z_LO) + z * CORES + lax.rem(e, CORES)

    order = [(4, 1), (4, 0), (0, 1), (1, 1), (3, 0), (7, 1), (5, 0), (2, 1), (2, 0), (6, 1), (6, 0), (3, 1), (1, 0), (5, 1), (7, 0)]
    partners = [lax.rem(y + far + core * (2 * rings - 2 * far), rings) * 2 + lax.rem(z_hi + other, 2) for far, other in order]
    levels = [lax.rem(z_lo + k, Z_LO) for k in range(1, Z_LO)]

    loads = [
        pltpu.make_async_copy(source, target, in_sem.at[i])
        for i, (source, target) in enumerate(
            ((plan_hbm, plan_ref), (orb_hbm, orb_ref), (table_hbm, table_ref), (mask_hbm, mask_ref))
        )
    ]
    for load in loads:
        load.start()

    barrier = pltpu.get_barrier_semaphore()
    greeted = [(device(lax.rem(x + k, RING_X) * CORES + core, z_lo), plane) for k in range(1, RING_X)]
    greeted += [(device(x * CORES + 1 - core, z_lo), plane)]
    greeted += [(device(here, z), plane) for z in levels]
    greeted += [(band, q) for q in partners]
    column = [
        (device(x * CORES + lax.rem(core + k % CORES, CORES), lax.rem(z_lo + k // CORES % Z_LO, Z_LO)),
         2 * y + lax.rem(z_hi + k // (CORES * Z_LO), 2))
        for k in range(1, 2 * CORES * Z_LO)
    ]
    greeted += [column[k - 1] for k in range(1, 2 * CORES * Z_LO) if k % CORES and k != 1 or k > CORES * Z_LO and k % CORES == 0]
    for target in greeted:
        pl.semaphore_signal(barrier, inc=1, device_id=target, device_id_type=MESH)

    loads[0].wait()
    loads[1].wait()
    def times_table(field, exact=False):
        left = jnp.concatenate(terms(field, False, exact), axis=1)
        right = jnp.concatenate(terms(table_ref[...], True, exact), axis=0)
        return jnp.dot(left, right, preferred_element_type=F32)

    def table_times(field, exact=False):
        left = jnp.concatenate(terms(table_ref[...], True, exact), axis=1)
        right = jnp.concatenate(terms(field, False, exact), axis=0)
        return jnp.dot(left, right, preferred_element_type=F32)

    def candidate(s):
        first = (plan_ref[s] == 2 * band).astype(F32)
        second = (plan_ref[s] == 2 * band + 1).astype(F32)
        chosen = orb_ref[0] * first + orb_ref[1] * second
        cand[s] = chosen.reshape(cand.shape[1:])

    candidate(0)
    pl.semaphore_wait(barrier, len(greeted))

    def copy(src, dst, send, recv, target):
        return pltpu.make_async_remote_copy(
            src_ref=src, dst_ref=dst, send_sem=send, recv_sem=recv, device_id=target, device_id_type=MESH
        )

    def rows(start, count):
        return pl.ds(pl.multiple_of(start, 8), count)

    def wait_rows(sem, count):
        ref = orb_ref.at[0, pl.ds(0, count)]
        pltpu.make_async_copy(ref, ref, sem).wait()

    piece = size // RING_X
    part = piece // Z_LO
    twin = (device(x * CORES + 1 - core, z_lo), plane)
    own_rows = rows(x * piece, piece)

    def core_copy(s):
        return copy(cand.at[s, :, 1 - core], crossed.at[s], core_send.at[s], core_recv.at[s], twin)

    def mix(s):
        core_copy(s).wait_recv()
        mixed[s] = cand[s, :, core] + crossed[s]

    def spread_out(i):
        s, j0, nj = phi_parts[i]
        js = pl.ds(j0, nj)
        for k in range(1, RING_X):
            to = lax.rem(x + k, RING_X)
            copy(
                mixed.at[s, js, rows(to * piece, piece)], spread.at[s, js, x],
                spread_send.at[i], spread_recv.at[i], (device(to * CORES + core, z_lo), plane),
            ).start()
        spread[s, js, x] = mixed[s, js, own_rows]

    def reduce_z(i):
        s, j0, nj = phi_parts[i]
        js = pl.ds(j0, nj)
        wait_rows(spread_recv.at[i], (RING_X - 1) * nj * piece)
        total = spread[s, js, 0]
        for k in range(1, RING_X):
            total = total + spread[s, js, k]
        reduced[s, js] = total
        for z in levels:
            copy(
                reduced.at[s, js, rows(z * part, part)], summed.at[s, js, z_lo],
                z_send.at[i], z_recv.at[i], (device(here, z), plane),
            ).start()
        summed[s, js, z_lo] = reduced[s, js, rows(z_lo * part, part)]

    def gather_z(i):
        s, j0, nj = phi_parts[i]
        js = pl.ds(j0, nj)
        wait_rows(z_recv.at[i], (Z_LO - 1) * nj * part)
        total = summed[s, js, 0]
        for k in range(1, Z_LO):
            total = total + summed[s, js, k]
        finest = rows(x * piece + z_lo * part, part)
        phi[s, js, core, finest] = total
        for z in levels:
            where = phi.at[s, js, core, finest]
            copy(where, where, up_send.at[i], up_recv.at[i], (device(here, z), plane)).start()

    def gather_x(i):
        s, j0, nj = phi_parts[i]
        js = pl.ds(j0, nj)
        wait_rows(up_recv.at[i], (Z_LO - 1) * nj * part)
        if i == len(phi_parts) - 1:
            for target in column:
                pl.semaphore_signal(calm, inc=1, device_id=target, device_id_type=MESH)
        for k in range(1, RING_X):
            where = phi.at[s, js, core, own_rows]
            to = (device(lax.rem(x + k, RING_X) * CORES + core, z_lo), plane)
            copy(where, where, gath_send.at[i], gath_recv.at[i], to).start()

    def half_copy(i):
        s, j0, nj = phi_parts[i]
        where = phi.at[s, pl.ds(j0, nj), core]
        return copy(where, where, half_send.at[i], half_recv.at[i], twin)

    def gather_core(i):
        wait_rows(gath_recv.at[i], (RING_X - 1) * phi_parts[i][2] * piece)
        half_copy(i).start()

    def all_calm():
        pl.semaphore_wait(calm, len(column))

    def have_phi(i):
        half_copy(i).wait_recv()

    def phi_rows(s, x0, nx):
        return phi[s, pl.ds(x0 // CORES, nx // CORES)].reshape(nx * size, size)

    def wait_blocks(sem, count):
        ref = landed.at[0, 0, pl.ds(0, count)]
        pltpu.make_async_copy(ref, ref, sem).wait()

    own = pl.ds(pl.multiple_of(plane * slab, slab), slab)

    def pair(i):
        s, x0, nx, b0, nb = pair_parts[i]
        for b in range(b0, b0 + nb):
            field = orb_ref[b, pl.ds(x0 * size, nx * size)] * phi_rows(s, x0, nx)
            field = times_table(field, exact=True)
            field = jnp.concatenate([field[j * size : (j + 1) * size] for j in range(nx)], axis=1)
            field = table_times(field, exact=True)
            for j in range(nx):
                sent[s, b, x0 + j] = field[:, j * size : (j + 1) * size]
        for b in range(b0, b0 + nb):
            landed[s, b, pl.ds(plane * slab + x0, nx)] = sent[s, b, pl.ds(x0, nx), own]

    def send_pair(i, targets):
        s, x0, nx, b0, nb = pair_parts[i]
        for q in targets:
            copy(
                sent.at[s, pl.ds(b0, nb), pl.ds(x0, nx), pl.ds(pl.multiple_of(q * slab, slab), slab)],
                landed.at[s, pl.ds(b0, nb), pl.ds(plane * slab + x0, nx)],
                fwd_send.at[i], fwd_recv.at[i], (band, q),
            ).start()

    arrived = set()

    def middle(s, b):
        for i, (s1, _, nx, b0, nb) in enumerate(pair_parts):
            if s1 == s and b0 <= b < b0 + nb and i not in arrived:
                arrived.add(i)
                wait_blocks(fwd_recv.at[i], (planes - 1) * nx * nb)
        source = landed.at[s, b].reshape(size * slab, size)
        target = filtered.at[s, b].reshape(size * slab, size)
        field = jnp.concatenate([source[pl.ds(k, size, stride=slab), :] for k in range(slab)], axis=1)
        field = table_times(field, exact=True) * filt[...]
        field = table_times(field)
        for k in range(slab):
            target[pl.ds(k, size, stride=slab), :] = field[:, k * size : (k + 1) * size]
        r = (0, 3, 7, 11)[s * bands + b]
        for q in partners[r:] + partners[:r]:
            copy(
                filtered.at[s, b, pl.ds(pl.multiple_of(q * slab, slab), slab)], returned.at[s, b, :, own],
                back_send.at[s, b], back_recv.at[s, b], (band, q),
            ).start()
        returned[s, b, :, own] = filtered[s, b, own]

    def last(s, b):
        wait_blocks(back_recv.at[s, b], (planes - 1) * slab)
        field = table_times(jnp.concatenate([returned[s, b, j] for j in range(slab)], axis=1))
        field = jnp.concatenate([field[:, j * size : (j + 1) * size] for j in range(slab)], axis=0)
        field = times_table(field) * phi_rows(s, 0, slab)
        out_ref[b] = field if s == 0 else out_ref[b] + field

    def screen():
        loads[2].wait()
        loads[3].wait()
        row = lax.broadcasted_iota(jnp.int32, (size, size), 0)
        col = lax.broadcasted_iota(jnp.int32, (size, size), 1)

        def wave(index, cell):
            return jnp.where(index < size // 2, index, index - size).astype(F32) * (2.0 * math.pi / cell)

        wave_ac = wave(row, 41.04) ** 2 + wave(col, 20.52) ** 2
        for k in range(slab):
            wave_b = wave(jnp.full((size, size), plane * slab + k, jnp.int32), 41.04)
            squared = wave_ac + wave_b * wave_b
            safe = jnp.where(squared > 0, squared, 1.0)
            screened = -4.0 * math.pi * (1.0 - jnp.exp(-safe / (4.0 * OMEGA * OMEGA))) / safe
            screened = jnp.where(squared > 0, screened, -math.pi / (OMEGA * OMEGA))
            keep = mask_ref[pl.ds(k, size, stride=slab), :].astype(F32)
            filt[:, k * size : (k + 1) * size] = screened * keep * (1.0 / (size * size * size))

    core_copy(0).start()
    candidate(1)
    core_copy(1).start()
    mix(0)
    spread_out(0)
    spread_out(1)
    mix(1)
    spread_out(2)
    screen()
    reduce_z(0)
    reduce_z(1)
    reduce_z(2)
    gather_z(0)
    gather_z(1)
    gather_z(2)
    gather_x(0)
    gather_x(1)
    gather_x(2)
    gather_core(0)
    gather_core(1)
    have_phi(0)
    have_phi(1)
    pair(0)
    all_calm()
    send_pair(0, partners)
    pair(1)
    send_pair(1, partners[3:] + partners[:3])
    gather_core(2)
    have_phi(2)
    pair(2)
    send_pair(2, partners[7:] + partners[:7])
    pair(3)
    send_pair(3, partners[11:] + partners[:11])
    units = [(s, b) for s in range(steps) for b in range(bands)]
    for unit in units:
        middle(*unit)
    for s in range(steps):
        core_copy(s).wait_send()
    for i, (_, _, nj) in enumerate(phi_parts):
        wait_rows(spread_send.at[i], (RING_X - 1) * nj * piece)
        wait_rows(z_send.at[i], (Z_LO - 1) * nj * part)
        wait_rows(up_send.at[i], (Z_LO - 1) * nj * part)
        wait_rows(gath_send.at[i], (RING_X - 1) * nj * piece)
        half_copy(i).wait_send()
    for i, (_, _, nx, _, nb) in enumerate(pair_parts):
        wait_blocks(fwd_send.at[i], (planes - 1) * nx * nb)
    for unit in units:
        last(*unit)
    for unit in units:
        wait_blocks(back_send.at[unit], (planes - 1) * slab)


def body(planes, orbitals, plan, cutoff_mask):
    bands, slab, size = orbitals.shape[:3]
    steps = plan.shape[0]
    phi_parts = [(0, 0, 2), (0, 2, 2), (1, 0, 4)]
    pair_parts = [(0, 0, 8, 0, 1), (0, 0, 8, 1, 1), (1, 0, 8, 0, 1), (1, 0, 8, 1, 1)]
    hbm = pl.BlockSpec(memory_space=pltpu.HBM)
    vmem = pltpu.VMEM
    dma = pltpu.SemaphoreType.DMA
    unit = (steps, bands)
    planes_per_core = slab // CORES
    parts, pairs = len(phi_parts), len(pair_parts)
    out = pl.pallas_call(
        functools.partial(kernel, planes, steps, bands, size, slab, phi_parts, pair_parts),
        out_shape=jax.ShapeDtypeStruct((bands, slab * size, size), F32),
        in_specs=[hbm, hbm, hbm, hbm],
        out_specs=pl.BlockSpec(memory_space=vmem),
        scratch_shapes=[
            pltpu.SMEM((steps,), jnp.int32),
            vmem((bands, slab * size, size), F32),
            vmem((size * slab, size), jnp.int32),
            vmem((size, size), F32),
            vmem((size, slab * size), F32),
            vmem((steps, planes_per_core, CORES, size, size), F32),
            vmem((steps, planes_per_core, size, size), F32),
            vmem((steps, planes_per_core, size, size), F32),
            vmem((steps, planes_per_core, RING_X, size // RING_X, size), F32),
            vmem((steps, planes_per_core, size // RING_X, size), F32),
            vmem((steps, planes_per_core, Z_LO, size // RING_X // Z_LO, size), F32),
            vmem((steps, planes_per_core, CORES, size, size), F32),
            vmem(unit + (slab, size, size), F32),
            vmem(unit + (size, slab, size), F32),
            vmem(unit + (size, slab, size), F32),
            vmem(unit + (slab, size, size), F32),
            pltpu.SemaphoreType.REGULAR,
            dma((4,)), dma((steps,)), dma((steps,)),
            *(dma((parts,)) for _ in range(10)),
            dma((pairs,)), dma((pairs,)),
            dma(unit), dma(unit),
        ],
        compiler_params=pltpu.CompilerParams(
            collective_id=0, has_side_effects=True, vmem_limit_bytes=40 * 2**20
        ),
    )(
        *(
            pltpu.with_memory_space_constraint(value, pltpu.HBM)
            for value in (
                plan,
                orbitals.reshape(bands, slab * size, size),
                cutoff_mask.reshape(size * slab, size),
                jnp.asarray(cas_table(size)),
            )
        )
    )
    return out.reshape(orbitals.shape)


def solution(mesh):
    return jax.shard_map(
        functools.partial(body, mesh.shape["plane"]),
        mesh=mesh,
        in_specs=(P("band", "plane", None, None), P(), P(None, "plane", None)),
        out_specs=P("band", "plane", None, None),
        check_vma=False,
    )
```
